256 devices in a mesh: section: 2 (over core), heads: 16 (over x, z_hi), rows: 8 (over z_lo, y).
Axes of the slice: x: 4, y: 4, z: 8 (z_hi: 4, z_lo: 2; z = z_hi * 2 + z_lo), core: 2. Of those that a mesh axis runs over, the one named last changes fastest.
Arguments:
- queries: bfloat16 [2, 8, 2048, 8192], P('section', 'rows', None, 'heads'), may hold values from -80 to 80
- keys_values: bfloat16 [2, 8, 2048, 2048], P('section', 'rows', None, 'heads'), may hold values from -4 to 4
- lengths: int32 [8], replicated, may hold values from 512 to 2048, as said below
- owners: int32 [128, 1], replicated, may hold values from 0 to 7; in each aligned block of 16 rows (0 to 15, 16 to 31, ...) at most 4 rows name the same one
Outputs:
- context: bfloat16 [2, 8, 2048, 8192], P('section', 'rows', None, 'heads')
- kv_pages: bfloat16 [8, 32, 128, 2048], P('rows', None, None, 'heads')
The draws below stay inside these ranges and needn't reach their ends.
Inputs may be any that keep to these rules, and one draw needn't show every extreme that they name: `lengths`: one prompt in every draw has length 2048. `owners`: among the 16 blocks of one prompt at most 4 have the same owner, and in every draw some owner receives exactly 4 blocks of some prompt.
All inputs are finite; a program needn't handle non-finite values.
Results may differ from the reference program's by a relative error of at most 0.0045.
Values may be sent and summed in bfloat16 or wider, within the bound.
No kernel may reach another device: no remote copies, remote signals or barrier semaphores. Data moves between devices by JAX's collectives and lax.ppermute only.
A program may use at most 128 MiB of HBM per device.

```python
import math
import jax
import jax.numpy as jnp
import numpy as np
from jax import lax

QH = 64
KVH = 8
HD = 128
LMAX = 2048
STEPS = 4
BLOCK = 128
PROMPTS = 8
NBLK = 16
CAP = 4
N_ROWS = 8


def anchor_keys(key):
    base_rows = jnp.clip(jax.random.normal(key, (2, PROMPTS, LMAX, KVH, HD), jnp.float32), -4.0, 4.0)
    even_rows = (jnp.arange(LMAX) % 2 == 0)[None, None, :, None, None]
    return jnp.where(even_rows, base_rows, base_rows)


def draw_keys_values(key, part):
    anchor = anchor_keys(key)
    key = jax.random.fold_in(key, 11)
    grid_shape = (2, PROMPTS, LMAX, KVH, HD)
    value_rows = jnp.clip(jax.random.normal(key, grid_shape, jnp.float32), -4.0, 4.0)
    paired = jnp.stack([anchor, value_rows], axis=4)
    return paired.reshape(2, PROMPTS, LMAX, KVH * 2 * HD).astype(jnp.bfloat16)


def draw_queries(key, part):
    anchor = anchor_keys(key)
    key = jax.random.fold_in(key, 5)
    noise_key = jax.random.fold_in(key, 0)
    grid_shape = (2, PROMPTS, LMAX, KVH, QH // KVH, HD)
    noise_rows = jnp.clip(jax.random.normal(noise_key, grid_shape, jnp.float32), -4.0, 4.0)
    strength = jnp.full((2, PROMPTS, LMAX), 0.5, jnp.float32)
    query_rows = noise_rows + strength[:, :, :, None, None, None] * anchor[:, :, :, :, None, :]
    query_rows = jnp.clip(query_rows, -80.0, 80.0)
    return query_rows.reshape(2, PROMPTS, LMAX, QH * HD).astype(jnp.bfloat16)


def draw_lengths(key, part):
    key = jax.random.fold_in(key, 3)
    draw_key, pick_key = jax.random.split(key)
    prompt_lengths = jax.random.randint(draw_key, (PROMPTS,), LMAX // 4, LMAX + 1)
    longest = jax.random.randint(pick_key, (), 0, PROMPTS)
    return jnp.where(jnp.arange(PROMPTS) == longest, LMAX, prompt_lengths).astype(jnp.int32)


def shared_out(stream_key, own, number, rows, number_of, top, most, skew):
    order = jax.random.permutation(stream_key, number_of)
    packed, usual = load_shares(number_of, rows * top, most, skew, True), load_shares(number_of, rows * top, most, skew, False)
    places = jnp.arange(number_of)

    def named(sizes, rotation):
        used = int((sizes > 0).sum())
        fixed = max(1, used // 4)
        moved = fixed + (places - fixed + rotation * (used - fixed)) % max(1, number_of - fixed)
        return jnp.zeros((number_of,), jnp.int32).at[order[jnp.where(places < fixed, places, moved)]].set(jnp.asarray(sizes, jnp.int32))

    sizes = jnp.where(number % 4 == 0, named(packed, number // 4), named(usual, number - number // 4 - 1))
    mixed = jax.random.permutation(jax.random.fold_in(own, 3), number_of)
    giver, receiver = mixed[0:number_of // 2 * 2:2], mixed[1:number_of // 2 * 2:2]
    room = jnp.minimum(sizes[giver] - 1, most - sizes[receiver]) // 2
    room = jnp.where((giver == order[0]) | (receiver == order[0]) | (sizes[receiver] == 0), 0, jnp.maximum(room, 0))
    moved = jax.random.randint(jax.random.fold_in(own, 4), (number_of // 2,), 0, 1 << 20) % (room + 1)
    sizes = sizes.at[giver].add(-moved).at[receiver].add(moved)
    members = jnp.searchsorted(jnp.cumsum(sizes), jnp.arange(rows * top), side="right").astype(jnp.int32)
    listing = members.reshape(top, rows).T
    listing = listing[jax.random.permutation(jax.random.fold_in(own, 1), rows)]
    rotation = jax.random.randint(jax.random.fold_in(own, 2), (rows, 1), 0, top)
    return jnp.take_along_axis(listing, (jnp.arange(top)[None, :] + rotation) % top, axis=1)


def load_shares(amount, total, limit, skew, full):
    portions = [(1 << 20) // math.isqrt(rank ** skew) + 1 for rank in range(1, amount + 1)]
    largest = limit if full else min(limit, max(-(-total // amount), total * portions[0] // sum(portions)))
    least = 1 if total - largest >= amount - 1 else 0
    given, surplus = [largest] + [least] * (amount - 1), total - largest - least * (amount - 1)
    while surplus > 0:
        free = [i for i in range(1, amount) if given[i] < largest] or [i for i in range(1, amount) if given[i] < limit]
        mass, left = sum([portions[i] for i in free]), surplus
        for i in free:
            addition = min(limit - given[i], max(1, left * portions[i] // mass), surplus)
            given[i] = given[i] + addition
            surplus = surplus - addition
    return np.array(given)


def setup_inputs(seed: int = 0) -> dict:
    key_of = jax.random.split(jax.random.key(seed), 5)
    queries = draw_queries(jax.random.fold_in(key_of[4], 71), 0)
    keys_values = draw_keys_values(jax.random.fold_in(key_of[4], 71), 0)
    lengths = draw_lengths(jax.random.fold_in(key_of[4], 71), 0)
    owners_keys = jax.random.split(jax.random.fold_in(key_of[3], 1), (PROMPTS * NBLK) // NBLK)
    owners_turns = jax.random.permutation(jax.random.fold_in(key_of[3], 3), (PROMPTS * NBLK) // NBLK)
    owners = jax.vmap(lambda own, number: shared_out(jax.random.fold_in(key_of[3], 2), own, number, NBLK, N_ROWS, 1, CAP, 1))(owners_keys, owners_turns).reshape((PROMPTS * NBLK, 1))
    return dict(queries=queries, keys_values=keys_values, lengths=lengths, owners=owners)


def weighted_context(query_heads, key_rows, value_rows, visible):
    score_scale = 1.0 / math.sqrt(HD)
    scores = jnp.einsum('gqd,kd->gqk', query_heads, key_rows) * score_scale
    scores = jnp.where(visible[None], scores, -jnp.inf)
    highest = lax.optimization_barrier(jnp.max(scores, axis=-1, keepdims=True))
    weights = jnp.exp(scores - highest)
    totals = lax.optimization_barrier(jnp.sum(weights, axis=-1, keepdims=True))
    rounded = lax.optimization_barrier(weights.astype(jnp.bfloat16)).astype(query_heads.dtype)
    return jnp.einsum('gqk,kd->gqd', rounded, value_rows) / totals

def split_queries(query_rows, seq_len):
    shaped = query_rows.astype(jnp.float32).reshape(seq_len, KVH, QH // KVH, HD)
    return shaped.transpose(1, 2, 0, 3)

def split_pairs(pair_rows, seq_len):
    shaped = pair_rows.astype(jnp.float32).reshape(seq_len, KVH, 2, HD).transpose(1, 2, 0, 3)
    return (shaped[:, 0], shaped[:, 1])

def merge_heads(context, seq_len):
    return context.transpose(2, 0, 1, 3).reshape(seq_len, QH * HD)

def reference(queries, keys_values, lengths, owners):
    seq_len = LMAX
    positions = jnp.arange(seq_len, dtype=jnp.int32)
    later = positions[:, None]
    earlier = positions[None, :]

    def prefill_prompt(operands):
        prompt_queries, prompt_pairs, length = operands
        visible = (earlier <= later) & ((earlier < length) | (earlier == later))
        key_heads, value_heads = split_pairs(prompt_pairs, seq_len)

        def per_head(head_operands):
            query_heads, key_rows, value_rows = head_operands
            return weighted_context(query_heads, key_rows, value_rows, visible)
        context = lax.map(per_head, (split_queries(prompt_queries, seq_len), key_heads, value_heads))
        context = merge_heads(context, seq_len)
        context = jnp.where((positions < length)[:, None], context, jnp.zeros_like(context))
        return context.astype(jnp.bfloat16)

    def decode_prompt(operands):
        decode_queries, decode_pairs, prompt_pairs, length = operands
        prompt_visible = jnp.broadcast_to(earlier < length, (seq_len, seq_len))
        own_visible = (earlier // STEPS == later // STEPS) & (earlier % STEPS <= later % STEPS)
        visible = jnp.concatenate([prompt_visible, own_visible], axis=1)
        prompt_keys, prompt_values = split_pairs(prompt_pairs, seq_len)
        own_keys, own_values = split_pairs(decode_pairs, seq_len)
        key_heads = jnp.concatenate([prompt_keys, own_keys], axis=1)
        value_heads = jnp.concatenate([prompt_values, own_values], axis=1)

        def per_head(head_operands):
            query_heads, key_rows, value_rows = head_operands
            return weighted_context(query_heads, key_rows, value_rows, visible)
        context = lax.map(per_head, (split_queries(decode_queries, seq_len), key_heads, value_heads))
        return merge_heads(context, seq_len).astype(jnp.bfloat16)
    prefill = lax.map(prefill_prompt, (queries[0], keys_values[0], lengths))
    decode = lax.map(decode_prompt, (queries[1], keys_values[1], keys_values[0], lengths))
    context = jnp.stack([prefill, decode])
    block_count = seq_len // BLOCK
    pair_width = 2 * KVH * HD
    prompt_pairs = keys_values[0]
    inside = (positions[None, :] < lengths[:, None])[:, :, None]
    kept_rows = jnp.where(inside, prompt_pairs, jnp.zeros_like(prompt_pairs))
    blocks = kept_rows.reshape(PROMPTS * block_count, BLOCK, pair_width)
    block_owner = owners[:, 0]
    block_ids = jnp.arange(PROMPTS * block_count, dtype=jnp.int32)
    source = block_ids // block_count
    before = (block_owner[:, None] == block_owner[None, :]) & (source[:, None] == source[None, :]) & (block_ids[None, :] < block_ids[:, None])
    block_rank = lax.optimization_barrier(jnp.sum(before.astype(jnp.int32), axis=1)).astype(jnp.int32)
    kv_pages = jnp.zeros((PROMPTS, PROMPTS * CAP, BLOCK, pair_width), keys_values.dtype)
    kv_pages = kv_pages.at[block_owner, source * CAP + block_rank].set(blocks)
    return (context, kv_pages)
```

```python
import functools
import math

import jax
import jax.numpy as jnp
from jax import lax
from jax.experimental import pallas as pl
from jax.experimental.pallas import tpu as pltpu
from jax.sharding import PartitionSpec as P

HD = 128
STEPS = 4
BLOCK = 128
ROWS = 512
KEYS = 256
LOW = -1e30
SCALE2 = math.log2(math.e) / math.sqrt(HD)
VMEM_LIMIT = 58 * 2**20

f32, bf16 = jnp.float32, jnp.bfloat16


def pages_kernel(block_count, capacity, lengths, owners, mine, shifted, buffer):
    role, group = lax.axis_index("section"), lax.axis_index("rows")
    length = lengths[group]
    buffer[...] = jnp.zeros_like(buffer)
    first = group * block_count
    named = [owners[first + b] for b in range(block_count)]

    def place(source):
        for b in range(block_count):
            rank = sum([(named[c] == named[b]).astype(jnp.int32) for c in range(b)], jnp.int32(0))
            at = b * BLOCK + lax.broadcasted_iota(jnp.int32, (BLOCK, 1), 0)
            rows = source[b * BLOCK : (b + 1) * BLOCK, :]
            buffer[named[b] * capacity + rank] = jnp.where(at < length, rows, jnp.zeros_like(rows))

    pl.when(role == 0)(lambda: place(mine))
    pl.when(role == 1)(lambda: place(shifted))


def scores_of(q, keys):
    return lax.dot_general(q, keys, (((1,), (1,)), ((), ())), preferred_element_type=f32)


def weights_of(scores, highest):
    wide = jnp.concatenate([highest] * (scores.shape[1] // HD), axis=1)
    return jnp.exp2((scores - wide) * SCALE2).astype(bf16)


def stage(keys, values, at, count, even_half, odd_half, parity, limit):
    index = at + lax.broadcasted_iota(jnp.int32, (count, 1), 0)
    inside = index < limit

    def fill(key_half, value_half):
        k, v = key_half[...], value_half[...]
        keys[at : at + count, :] = jnp.where(inside, k, jnp.broadcast_to(k[0:1], k.shape))
        values[at : at + count, :HD] = jnp.where(inside, v, jnp.zeros_like(v))
        values[at : at + count, HD:] = jnp.broadcast_to(jnp.where(inside, 1.0, 0.0), v.shape).astype(bf16)

    pl.when(parity == 0)(lambda: fill(even_half, odd_half))
    pl.when(parity == 1)(lambda: fill(odd_half, even_half))


def step(state, scores, rows_of_values):
    highest = jnp.broadcast_to(jnp.max(scores, axis=1, keepdims=True), (scores.shape[0], HD))
    if state is None:
        return highest, rows_of_values(weights_of(scores, highest))
    old, summed = state
    highest = jnp.maximum(old, highest)
    factor = jnp.exp2((old - highest) * SCALE2)
    return highest, summed * jnp.concatenate([factor, factor], axis=1) + rows_of_values(weights_of(scores, highest))


def weighted(values):
    return lambda weights: jnp.dot(weights, values, preferred_element_type=f32)


def key_blocks(state, q, keys, values, first, last):
    for at in range(first, last, KEYS):
        state = step(state, scores_of(q, keys[at : at + KEYS, :]), weighted(values[at : at + KEYS, :]))
    return state


def finished(summed):
    return summed[:, :HD] / summed[:, HD:]


def prefill_rows(block, q, keys, values, length, out):
    at = block * ROWS
    diagonal = lax.broadcasted_iota(jnp.int32, (ROWS, KEYS), 1) <= lax.broadcasted_iota(jnp.int32, (ROWS, KEYS), 0)
    live = at + lax.broadcasted_iota(jnp.int32, (ROWS, 1), 0) < length
    for j in range(q.shape[1] // HD):
        rows = q[:, j * HD : (j + 1) * HD]
        state = key_blocks(None, rows, keys, values, 0, at)
        done = []
        for n in range(0, ROWS, KEYS):
            scores = jnp.where(diagonal[: ROWS - n], scores_of(rows[n:], keys[at + n : at + n + KEYS, :]), LOW)
            state = step(state, scores, weighted(values[at + n : at + n + KEYS, :]))
            done.append(finished(state[1][:KEYS]))
            state = tuple(x[KEYS:] for x in state)
        context = jnp.concatenate(done, axis=0)
        out[:, j * HD : (j + 1) * HD] = jnp.where(live, context, 0.0).astype(bf16)


def first_kernel(half, lengths, q, mine, across, shifted, shifted_across, ctx, acc, top, keys, values):
    i = pl.program_id(0)
    role, parity = lax.axis_index("section"), lax.axis_index("heads") & 1
    length = lengths[lax.axis_index("rows")]

    @pl.when(i == 0)
    def _():
        far = jnp.int32(2**30)
        pl.when(role == 0)(lambda: stage(keys, values, 0, half, mine, across, parity, far))
        pl.when(role == 1)(lambda: stage(keys, values, 0, half, shifted, shifted_across, parity, length))

    for block in range(half // ROWS):

        @pl.when((role == 0) & (i == block))
        def _():
            prefill_rows(block, q, keys, values, length, ctx)

    @pl.when(role == 1)
    def _():
        heads = q.shape[1] // HD
        for j in range(heads):
            highest, summed = key_blocks(None, q[:, j * HD : (j + 1) * HD], keys, values, 0, half)
            acc[:, 2 * j * HD : 2 * (j + 1) * HD] = summed
            top[:, j * HD : (j + 1) * HD] = highest


def second_kernel(
    half, lengths, q, mine_a, across_a, mine_b, across_b, shifted_b, shifted_across_b,
    own_half, own_across, before, acc, top, arrived, ctx, pages, keys, values, own_keys, own_values, bias,
):
    i = pl.program_id(0)
    role, parity = lax.axis_index("section"), lax.axis_index("heads") & 1
    length = lengths[lax.axis_index("rows")]
    blocks = 2 * half // ROWS
    far = jnp.int32(2**30)
    pages[...] = arrived[...]

    @pl.when((i == 0) & (role == 0))
    def _():
        stage(keys, values, 0, half, mine_a, across_a, parity, far)
        stage(keys, values, half, half, mine_b, across_b, parity, far)

    @pl.when((i == 0) & (role == 1))
    def _():
        stage(keys, values, half, half, shifted_b, shifted_across_b, parity, length)
        rows_at = lax.broadcasted_iota(jnp.int32, (KEYS, KEYS), 0)
        cols_at = lax.broadcasted_iota(jnp.int32, (KEYS, KEYS), 1)
        visible = (rows_at // STEPS == cols_at // STEPS) & (cols_at <= rows_at)
        bias[...] = jnp.where(visible, 0.0, LOW)

    @pl.when((role == 0) & (i < blocks // 2))
    def _():
        ctx[...] = before[...]

    for block in range(blocks // 2, blocks):

        @pl.when((role == 0) & (i == block))
        def _():
            prefill_rows(block, q, keys, values, length, ctx)

    def decode(with_prompt):
        heads = q.shape[1] // HD
        parts = range(0, ROWS, KEYS)

        def own_weighted(weights):
            return jnp.concatenate([weighted(own_values[n : n + KEYS, :])(weights[n : n + KEYS]) for n in parts], axis=0)

        for j in range(heads):
            rows = q[:, j * HD : (j + 1) * HD]
            state = top[:, j * HD : (j + 1) * HD], acc[:, 2 * j * HD : 2 * (j + 1) * HD]
            if with_prompt:
                state = key_blocks(state, rows, keys, values, half, 2 * half)
            own = jnp.concatenate([scores_of(rows[n : n + KEYS], own_keys[n : n + KEYS, :]) for n in parts], axis=0)
            state = step(state, own + jnp.concatenate([bias[...]] * len(parts), axis=0), own_weighted)
            ctx[:, j * HD : (j + 1) * HD] = finished(state[1]).astype(bf16)

    @pl.when(role == 1)
    def _():
        stage(own_keys, own_values, 0, ROWS, own_half, own_across, parity, far)
        pl.when(length > half)(lambda: decode(True))
        pl.when(length <= half)(lambda: decode(False))

def after(value, *others):
    return lax.optimization_barrier((value, *others))[0]


def shards(queries, keys_values, lengths, owners):
    rows_count, pairs = lax.axis_size("rows"), lax.axis_size("heads")
    seq_len, width = keys_values.shape[2:]
    half = seq_len // 2
    block_count = seq_len // BLOCK
    capacity = 2 * block_count // rows_count
    mine = keys_values.reshape(seq_len, width)
    q = queries.reshape(seq_len, -1)
    q_width = q.shape[1]
    owners = owners.reshape(-1)

    def across(value, section):
        base = section * pairs
        return lax.ppermute(value, ("section", "heads"), [(base + h, base + (h ^ 1)) for h in range(pairs)])

    def shift(value):
        return lax.ppermute(value, "section", [(0, 1)])

    mine_a, mine_b = mine[:half], mine[half:]
    across_a = across(mine_a, 0)
    shifted = shift(mine)
    whole = pl.BlockSpec(memory_space=pltpu.VMEM)
    smem = pl.BlockSpec(memory_space=pltpu.SMEM)
    params = pltpu.CompilerParams(vmem_limit_bytes=VMEM_LIMIT)
    buffer = pl.pallas_call(
        functools.partial(pages_kernel, block_count, capacity),
        in_specs=[smem, smem, whole, whole],
        out_specs=whole,
        out_shape=jax.ShapeDtypeStruct((rows_count * capacity, BLOCK, width), bf16),
        compiler_params=params,
        cost_estimate=pl.CostEstimate(flops=20 * 10**9, bytes_accessed=2**26, transcendentals=0),
        name="pages",
    )(lengths, owners, mine, shifted)
    arrived = lax.all_to_all(
        buffer.reshape(rows_count, capacity, BLOCK, width), "rows", split_axis=0, concat_axis=0, tiled=True
    )
    arrived = arrived.reshape(1, -1, BLOCK, width)

    shifted_across_a = shift(across_a)
    across_b = across(after(mine_b, across_a), 0)
    shifted_across_b = shift(across_b)
    own_across = across(after(mine, across_b), 1)

    def rows_of(width):
        return pl.BlockSpec((ROWS, width), lambda i: (i, 0))

    def part(which):
        return pl.BlockSpec((half, width), lambda i: (which, 0))

    heads = q_width // HD
    flops = 4 * seq_len * half * q_width
    ctx, acc, top = pl.pallas_call(
        functools.partial(first_kernel, half),
        grid=(seq_len // ROWS,),
        in_specs=[smem, rows_of(q_width), part(0), part(0), part(0), part(0)],
        out_specs=[rows_of(q_width), rows_of(2 * q_width), rows_of(q_width)],
        out_shape=[
            jax.ShapeDtypeStruct((seq_len, q_width), bf16),
            jax.ShapeDtypeStruct((seq_len, 2 * q_width), f32),
            jax.ShapeDtypeStruct((seq_len, q_width), f32),
        ],
        scratch_shapes=[pltpu.VMEM((half, HD), bf16), pltpu.VMEM((half, 2 * HD), bf16)],
        compiler_params=params,
        cost_estimate=pl.CostEstimate(flops=flops, bytes_accessed=2**24, transcendentals=heads * seq_len * half),
        name="first_keys",
    )(lengths, q, mine, across_a, shifted, shifted_across_a)
    slots = rows_count * capacity
    page_part = pl.BlockSpec((1, slots * ROWS // seq_len, BLOCK, width), lambda i: (0, i, 0, 0))
    context, kv_pages = pl.pallas_call(
        functools.partial(second_kernel, half),
        grid=(seq_len // ROWS,),
        in_specs=[
            smem, rows_of(q_width), part(0), part(0), part(1), part(0), part(1), part(0),
            rows_of(width), rows_of(width), rows_of(q_width), rows_of(2 * q_width), rows_of(q_width), page_part,
        ],
        out_specs=[rows_of(q_width), page_part],
        out_shape=[
            jax.ShapeDtypeStruct((seq_len, q_width), bf16),
            jax.ShapeDtypeStruct((1, slots, BLOCK, width), bf16),
        ],
        scratch_shapes=[
            pltpu.VMEM((seq_len, HD), bf16),
            pltpu.VMEM((seq_len, 2 * HD), bf16),
            pltpu.VMEM((ROWS, HD), bf16),
            pltpu.VMEM((ROWS, 2 * HD), bf16),
            pltpu.VMEM((KEYS, KEYS), f32),
        ],
        compiler_params=params,
        cost_estimate=pl.CostEstimate(flops=flops, bytes_accessed=2**24, transcendentals=heads * seq_len * half),
        name="second_keys",
    )(lengths, q, mine, across_a, mine, across_b, shifted, shifted_across_b, mine, own_across, ctx, acc, top, arrived)
    return (context.reshape(1, 1, seq_len, -1), kv_pages)


def solution(mesh):
    in_specs = (P("section", "rows", None, "heads"), P("section", "rows", None, "heads"), P(), P())
    out_specs = (P("section", "rows", None, "heads"), P("rows", None, None, "heads"))
    return jax.shard_map(shards, mesh=mesh, in_specs=in_specs, out_specs=out_specs, check_vma=False)
```

```python
import functools
import math

import jax
import jax.numpy as jnp
from jax import lax
from jax.experimental import pallas as pl
from jax.experimental.pallas import tpu as pltpu
from jax.sharding import PartitionSpec as P

HD = 128
STEPS = 4
BLOCK = 128
ROWS = 512
KEYS = 256
LOW = -1e30
SCALE2 = math.log2(math.e) / math.sqrt(HD)
VMEM_LIMIT = 58 * 2**20

f32, bf16 = jnp.float32, jnp.bfloat16


def pages_kernel(block_count, capacity, lengths, owners, mine, shifted, buffer):
    role, group = lax.axis_index("section"), lax.axis_index("rows")
    length = lengths[group]
    buffer[...] = jnp.zeros_like(buffer)
    first = group * block_count
    named = [owners[first + b] for b in range(block_count)]

    def place(source):
        for b in range(block_count):
            rank = sum([(named[c] == named[b]).astype(jnp.int32) for c in range(b)], jnp.int32(0))
            at = b * BLOCK + lax.broadcasted_iota(jnp.int32, (BLOCK, 1), 0)
            rows = source[b * BLOCK : (b + 1) * BLOCK, :]
            buffer[named[b] * capacity + rank] = jnp.where(at < length, rows, jnp.zeros_like(rows))

    pl.when(role == 0)(lambda: place(mine))
    pl.when(role == 1)(lambda: place(shifted))


def scores_of(q, keys):
    return lax.dot_general(q, keys, (((1,), (1,)), ((), ())), preferred_element_type=f32)


def weights_of(scores, highest):
    wide = jnp.concatenate([highest] * (scores.shape[1] // HD), axis=1)
    return jnp.exp2((scores - wide) * SCALE2).astype(bf16)


def stage(keys, values, first_half, second_half, parity):
    def fill(key_half, value_half):
        keys[...] = key_half[...]
        values[:, :HD] = value_half[...]

    pl.when(parity == 0)(lambda: fill(first_half, second_half))
    pl.when(parity == 1)(lambda: fill(second_half, first_half))
    values[:, HD:] = jnp.ones((values.shape[0], HD), bf16)


def cut(keys, values, length):
    for at in range(0, keys.shape[0], BLOCK):
        span = slice(at, at + BLOCK)

        @pl.when(length < at + BLOCK)
        def _():
            inside = at + lax.broadcasted_iota(jnp.int32, (BLOCK, HD), 0) < length
            first = jnp.broadcast_to(keys[0:1, :].astype(f32), (BLOCK, HD))
            keys[span, :] = jnp.where(inside, keys[span, :].astype(f32), first).astype(bf16)
            values[span, :HD] = jnp.where(inside, values[span, :HD].astype(f32), 0.0).astype(bf16)
            values[span, HD:] = jnp.where(inside, 1.0, 0.0).astype(bf16)


def step(state, scores, rows_of_values):
    highest = jnp.broadcast_to(jnp.max(scores, axis=1, keepdims=True), (scores.shape[0], HD))
    if state is None:
        return highest, rows_of_values(weights_of(scores, highest))
    old, summed = state
    highest = jnp.maximum(old, highest)
    factor = jnp.exp2((old - highest) * SCALE2)
    return highest, summed * jnp.concatenate([factor, factor], axis=1) + rows_of_values(weights_of(scores, highest))


def weighted(values):
    return lambda weights: jnp.dot(weights, values, preferred_element_type=f32)


def key_blocks(state, q, keys, values, first, last):
    for at in range(first, last, KEYS):
        state = step(state, scores_of(q, keys[at : at + KEYS, :]), weighted(values[at : at + KEYS, :]))
    return state


def finished(summed):
    return summed[:, :HD] / summed[:, HD:]


def prefill_rows(block, q, keys, values, length, out):
    at = block * ROWS
    diagonal = lax.broadcasted_iota(jnp.int32, (ROWS, KEYS), 1) <= lax.broadcasted_iota(jnp.int32, (ROWS, KEYS), 0)
    live = at + lax.broadcasted_iota(jnp.int32, (ROWS, 1), 0) < length
    for j in range(q.shape[1] // HD):
        rows = q[:, j * HD : (j + 1) * HD]
        state = key_blocks(None, rows, keys, values, 0, at)
        done = []
        for n in range(0, ROWS, KEYS):
            scores = jnp.where(diagonal[: ROWS - n], scores_of(rows[n:], keys[at + n : at + n + KEYS, :]), LOW)
            state = step(state, scores, weighted(values[at + n : at + n + KEYS, :]))
            done.append(finished(state[1][:KEYS]))
            state = tuple(x[KEYS:] for x in state)
        context = jnp.concatenate(done, axis=0)
        out[:, j * HD : (j + 1) * HD] = jnp.where(live, context, 0.0).astype(bf16)


def decode_rows(q, keys, values, own_keys, own_values, bias, out):
    parts = range(0, ROWS, KEYS)

    def own_weighted(weights):
        return jnp.concatenate([weighted(own_values[n : n + KEYS, :])(weights[n : n + KEYS]) for n in parts], axis=0)

    for j in range(q.shape[1] // HD):
        rows = q[:, j * HD : (j + 1) * HD]
        own = jnp.concatenate([scores_of(rows[n : n + KEYS], own_keys[n : n + KEYS, :]) for n in parts], axis=0)
        state = step(None, own + jnp.concatenate([bias[...]] * len(parts), axis=0), own_weighted)
        state = key_blocks(state, rows, keys, values, 0, keys.shape[0])
        out[:, j * HD : (j + 1) * HD] = finished(state[1]).astype(bf16)


def attend_kernel(
    lengths, q, mine, across, shifted, shifted_across, own_half, own_across,
    ctx, keys, values, own_keys, own_values, bias,
):
    i = pl.program_id(0)
    role, parity = lax.axis_index("section"), lax.axis_index("heads") & 1
    length = lengths[lax.axis_index("rows")]

    @pl.when((i == 0) & (role == 0))
    def _():
        stage(keys, values, mine, across, parity)

    @pl.when((i == 0) & (role == 1))
    def _():
        stage(keys, values, shifted, shifted_across, parity)
        cut(keys, values, length)
        rows_at = lax.broadcasted_iota(jnp.int32, (KEYS, KEYS), 0)
        cols_at = lax.broadcasted_iota(jnp.int32, (KEYS, KEYS), 1)
        visible = (rows_at // STEPS == cols_at // STEPS) & (cols_at <= rows_at)
        bias[...] = jnp.where(visible, 0.0, LOW)

    for block in range(keys.shape[0] // ROWS):

        @pl.when((role == 0) & (i == block))
        def _():
            prefill_rows(block, q, keys, values, length, ctx)

    @pl.when(role == 1)
    def _():
        stage(own_keys, own_values, own_half, own_across, parity)
        decode_rows(q, keys, values, own_keys, own_values, bias, ctx)


def after(value, *others):
    return lax.optimization_barrier((value, *others))[0]


def shards(queries, keys_values, lengths, owners):
    rows_count, pairs = lax.axis_size("rows"), lax.axis_size("heads")
    seq_len, width = keys_values.shape[2:]
    block_count = seq_len // BLOCK
    capacity = 2 * block_count // rows_count
    mine = keys_values.reshape(seq_len, width)
    q = queries.reshape(seq_len, -1)
    q_width = q.shape[1]
    owners = owners.reshape(-1)

    def across(value, section):
        base = section * pairs
        return lax.ppermute(value, ("section", "heads"), [(base + h, base + (h ^ 1)) for h in range(pairs)])

    def shift(value):
        return lax.ppermute(value, "section", [(0, 1)])

    across_mine = across(mine, 0)
    shifted = shift(mine)
    whole = pl.BlockSpec(memory_space=pltpu.VMEM)
    smem = pl.BlockSpec(memory_space=pltpu.SMEM)
    params = pltpu.CompilerParams(vmem_limit_bytes=VMEM_LIMIT)
    buffer = pl.pallas_call(
        functools.partial(pages_kernel, block_count, capacity),
        in_specs=[smem, smem, whole, whole],
        out_specs=whole,
        out_shape=jax.ShapeDtypeStruct((rows_count * capacity, BLOCK, width), bf16),
        compiler_params=params,
        cost_estimate=pl.CostEstimate(flops=20 * 10**9, bytes_accessed=2**26, transcendentals=0),
        name="pages",
    )(lengths, owners, mine, shifted)
    arrived = lax.all_to_all(
        buffer.reshape(rows_count, capacity, BLOCK, width), "rows", split_axis=0, concat_axis=0, tiled=True
    )
    kv_pages = arrived.reshape(1, -1, BLOCK, width)

    shifted_across = shift(across_mine)
    own_across = across(after(mine, buffer), 1)

    def rows_of(width):
        return pl.BlockSpec((ROWS, width), lambda i: (i, 0))

    heads = q_width // HD
    context = pl.pallas_call(
        attend_kernel,
        grid=(seq_len // ROWS,),
        in_specs=[smem, rows_of(q_width), whole, whole, whole, whole, rows_of(width), rows_of(width)],
        out_specs=rows_of(q_width),
        out_shape=jax.ShapeDtypeStruct((seq_len, q_width), bf16),
        scratch_shapes=[
            pltpu.VMEM((seq_len, HD), bf16),
            pltpu.VMEM((seq_len, 2 * HD), bf16),
            pltpu.VMEM((ROWS, HD), bf16),
            pltpu.VMEM((ROWS, 2 * HD), bf16),
            pltpu.VMEM((KEYS, KEYS), f32),
        ],
        compiler_params=params,
        cost_estimate=pl.CostEstimate(flops=40 * 10**9, bytes_accessed=2**24, transcendentals=heads * seq_len**2),
        name="attend",
    )(lengths, q, mine, across_mine, shifted, shifted_across, mine, own_across)
    return (context.reshape(1, 1, seq_len, -1), kv_pages)


def solution(mesh):
    in_specs = (P("section", "rows", None, "heads"), P("section", "rows", None, "heads"), P(), P())
    out_specs = (P("section", "rows", None, "heads"), P("rows", None, None, "heads"))
    return jax.shard_map(shards, mesh=mesh, in_specs=in_specs, out_specs=out_specs, check_vma=False)
```

```python
import functools
import math

import jax
import jax.numpy as jnp
from jax import lax
from jax.experimental import pallas as pl
from jax.experimental.pallas import tpu as pltpu
from jax.sharding import PartitionSpec as P

HD = 128
STEPS = 4
BLOCK = 128
ROWS = 512
KEYS = 256
SPAN = 256
LOW = -1e30
SCALE2 = math.log2(math.e) / math.sqrt(HD)
VMEM_LIMIT = 58 * 2**20

f32, bf16 = jnp.float32, jnp.bfloat16


def pages_kernel(block_count, capacity, lengths, owners, mine, shifted, buffer):
    role, group = lax.axis_index("section"), lax.axis_index("rows")
    length = lengths[group]
    buffer[...] = jnp.zeros_like(buffer)
    first = group * block_count
    named = [owners[first + b] for b in range(block_count)]

    def place(source):
        for b in range(block_count):
            rank = sum([(named[c] == named[b]).astype(jnp.int32) for c in range(b)], jnp.int32(0))
            at = b * BLOCK + lax.broadcasted_iota(jnp.int32, (BLOCK, 1), 0)
            rows = source[b * BLOCK : (b + 1) * BLOCK, :]
            buffer[named[b] * capacity + rank] = jnp.where(at < length, rows, jnp.zeros_like(rows))

    pl.when(role == 0)(lambda: place(mine))
    pl.when(role == 1)(lambda: place(shifted))


def scores_of(q, keys):
    return lax.dot_general(q, keys, (((1,), (1,)), ((), ())), preferred_element_type=f32)


def weights_of(scores, highest):
    wide = jnp.concatenate([highest] * (scores.shape[1] // HD), axis=1)
    return jnp.exp2((scores - wide) * SCALE2).astype(bf16)


def stage(keys, values, first_half, second_half, parity):
    def fill(key_half, value_half):
        keys[...] = key_half[...]
        values[:, :HD] = value_half[...]

    pl.when(parity == 0)(lambda: fill(first_half, second_half))
    pl.when(parity == 1)(lambda: fill(second_half, first_half))
    values[:, HD:] = jnp.ones((values.shape[0], HD), bf16)


def cut(keys, values, length):
    for at in range(0, keys.shape[0], BLOCK):
        span = slice(at, at + BLOCK)

        @pl.when(length < at + BLOCK)
        def _():
            inside = at + lax.broadcasted_iota(jnp.int32, (BLOCK, HD), 0) < length
            first = jnp.broadcast_to(keys[0:1, :].astype(f32), (BLOCK, HD))
            keys[span, :] = jnp.where(inside, keys[span, :].astype(f32), first).astype(bf16)
            values[span, :HD] = jnp.where(inside, values[span, :HD].astype(f32), 0.0).astype(bf16)
            values[span, HD:] = jnp.where(inside, 1.0, 0.0).astype(bf16)


def step(state, scores, rows_of_values):
    highest = jnp.broadcast_to(jnp.max(scores, axis=1, keepdims=True), (scores.shape[0], HD))
    if state is None:
        return highest, rows_of_values(weights_of(scores, highest))
    old, summed = state
    highest = jnp.maximum(old, highest)
    factor = jnp.exp2((old - highest) * SCALE2)
    return highest, summed * jnp.concatenate([factor, factor], axis=1) + rows_of_values(weights_of(scores, highest))


def weighted(values):
    return lambda weights: jnp.dot(weights, values, preferred_element_type=f32)


def key_blocks(state, q, keys, values, first, last):
    for at in range(first, last, KEYS):
        state = step(state, scores_of(q, keys[at : at + KEYS, :]), weighted(values[at : at + KEYS, :]))
    return state


def finished(summed):
    return summed[:, :HD] / summed[:, HD:]


def prefill_rows(block, q, keys, values, length, out):
    at = block * ROWS
    diagonal = lax.broadcasted_iota(jnp.int32, (ROWS, KEYS), 1) <= lax.broadcasted_iota(jnp.int32, (ROWS, KEYS), 0)
    live = at + lax.broadcasted_iota(jnp.int32, (ROWS, 1), 0) < length
    for j in range(q.shape[1] // HD):
        rows = q[:, j * HD : (j + 1) * HD]
        state = key_blocks(None, rows, keys, values, 0, at)
        done = []
        for n in range(0, ROWS, KEYS):
            scores = jnp.where(diagonal[: ROWS - n], scores_of(rows[n:], keys[at + n : at + n + KEYS, :]), LOW)
            state = step(state, scores, weighted(values[at + n : at + n + KEYS, :]))
            done.append(finished(state[1][:KEYS]))
            state = tuple(x[KEYS:] for x in state)
        context = jnp.concatenate(done, axis=0)
        out[:, j * HD : (j + 1) * HD] = jnp.where(live, context, 0.0).astype(bf16)


def decode_rows(q, keys, values, own_keys, own_values, bias, out):
    heads = q.shape[1] // HD
    own = []
    for n in range(0, ROWS, SPAN):
        span = slice(n, n + SPAN)
        rows = jnp.concatenate([q[span, j * HD : (j + 1) * HD] for j in range(heads)], axis=0)
        scores = scores_of(rows, own_keys[span, :]) + jnp.concatenate([bias[...]] * heads, axis=0)
        own.append(step(None, scores, weighted(own_values[span, :])))
    for j in range(heads):
        span = slice(j * SPAN, (j + 1) * SPAN)
        state = tuple(jnp.concatenate([part[k][span] for part in own], axis=0) for k in range(2))
        state = key_blocks(state, q[:, j * HD : (j + 1) * HD], keys, values, 0, keys.shape[0])
        out[:, j * HD : (j + 1) * HD] = finished(state[1]).astype(bf16)


def attend_kernel(
    lengths, q, mine, across, shifted, shifted_across, own_half, own_across,
    ctx, keys, values, own_keys, own_values, bias,
):
    i = pl.program_id(0)
    role, parity = lax.axis_index("section"), lax.axis_index("heads") & 1
    length = lengths[lax.axis_index("rows")]

    @pl.when((i == 0) & (role == 0))
    def _():
        stage(keys, values, mine, across, parity)

    @pl.when((i == 0) & (role == 1))
    def _():
        stage(keys, values, shifted, shifted_across, parity)
        cut(keys, values, length)
        rows_at = lax.broadcasted_iota(jnp.int32, (SPAN, SPAN), 0)
        cols_at = lax.broadcasted_iota(jnp.int32, (SPAN, SPAN), 1)
        visible = (rows_at // STEPS == cols_at // STEPS) & (cols_at <= rows_at)
        bias[...] = jnp.where(visible, 0.0, LOW)

    for block in range(keys.shape[0] // ROWS):

        @pl.when((role == 0) & (i == block))
        def _():
            prefill_rows(block, q, keys, values, length, ctx)

    @pl.when(role == 1)
    def _():
        stage(own_keys, own_values, own_half, own_across, parity)
        decode_rows(q, keys, values, own_keys, own_values, bias, ctx)


def shards(queries, keys_values, lengths, owners):
    rows_count, pairs = lax.axis_size("rows"), lax.axis_size("heads")
    seq_len, width = keys_values.shape[2:]
    block_count = seq_len // BLOCK
    capacity = 2 * block_count // rows_count
    mine = keys_values.reshape(seq_len, width)
    q = queries.reshape(seq_len, -1)
    q_width = q.shape[1]
    owners = owners.reshape(-1)

    def to_partner(value, section):
        return lax.ppermute(
            value, ("section", "heads"), [(section * pairs + h, pairs + (h ^ 1)) for h in range(pairs)]
        )

    own_across = to_partner(mine, 1)
    shifted_across = to_partner(mine, 0)
    shifted = lax.ppermute(mine, "section", [(0, 1)])
    whole = pl.BlockSpec(memory_space=pltpu.VMEM)
    smem = pl.BlockSpec(memory_space=pltpu.SMEM)
    params = pltpu.CompilerParams(vmem_limit_bytes=VMEM_LIMIT)
    buffer = pl.pallas_call(
        functools.partial(pages_kernel, block_count, capacity),
        in_specs=[smem, smem, whole, whole],
        out_specs=whole,
        out_shape=jax.ShapeDtypeStruct((rows_count * capacity, BLOCK, width), bf16),
        compiler_params=params,
        cost_estimate=pl.CostEstimate(flops=20 * 10**9, bytes_accessed=2**26, transcendentals=0),
        name="pages",
    )(lengths, owners, mine, shifted)
    arrived = lax.all_to_all(
        buffer.reshape(rows_count, capacity, BLOCK, width), "rows", split_axis=0, concat_axis=0, tiled=True
    )
    kv_pages = arrived.reshape(1, -1, BLOCK, width)

    shifted_across, _ = lax.optimization_barrier((shifted_across, buffer))
    across_mine = lax.ppermute(shifted_across, "section", [(1, 0)])

    def rows_of(width):
        return pl.BlockSpec((ROWS, width), lambda i: (i, 0))

    heads = q_width // HD
    context = pl.pallas_call(
        attend_kernel,
        grid=(seq_len // ROWS,),
        in_specs=[smem, rows_of(q_width), whole, whole, whole, whole, rows_of(width), rows_of(width)],
        out_specs=rows_of(q_width),
        out_shape=jax.ShapeDtypeStruct((seq_len, q_width), bf16),
        scratch_shapes=[
            pltpu.VMEM((seq_len, HD), bf16),
            pltpu.VMEM((seq_len, 2 * HD), bf16),
            pltpu.VMEM((ROWS, HD), bf16),
            pltpu.VMEM((ROWS, 2 * HD), bf16),
            pltpu.VMEM((SPAN, SPAN), f32),
        ],
        compiler_params=params,
        cost_estimate=pl.CostEstimate(flops=11 * 10**9, bytes_accessed=2**20, transcendentals=0),
        name="attend",
    )(lengths, q, mine, across_mine, shifted, shifted_across, mine, own_across)
    return (context.reshape(1, 1, seq_len, -1), kv_pages)


def solution(mesh):
    in_specs = (P("section", "rows", None, "heads"), P("section", "rows", None, "heads"), P(), P())
    out_specs = (P("section", "rows", None, "heads"), P("rows", None, None, "heads"))
    return jax.shard_map(shards, mesh=mesh, in_specs=in_specs, out_specs=out_specs, check_vma=False)
```

```python
import functools
import math

import jax
import jax.numpy as jnp
from jax import lax
from jax.experimental import pallas as pl
from jax.experimental.pallas import tpu as pltpu
from jax.sharding import PartitionSpec as P

HD = 128
STEPS = 4
BLOCK = 128
ROWS = 512
KEYS = 256
SPAN = 256
EARLY = 2
FIRST_FLOPS = 14 * 10**9
LOW = -1e30
SCALE2 = math.log2(math.e) / math.sqrt(HD)
VMEM_LIMIT = 58 * 2**20

f32, bf16 = jnp.float32, jnp.bfloat16


def pages_kernel(block_count, capacity, lengths, owners, mine, shifted, buffer):
    role, group = lax.axis_index("section"), lax.axis_index("rows")
    length = lengths[group]
    buffer[...] = jnp.zeros_like(buffer)
    first = group * block_count
    named = [owners[first + b] for b in range(block_count)]

    def place(source):
        for b in range(block_count):
            rank = sum([(named[c] == named[b]).astype(jnp.int32) for c in range(b)], jnp.int32(0))
            at = b * BLOCK + lax.broadcasted_iota(jnp.int32, (BLOCK, 1), 0)
            rows = source[b * BLOCK : (b + 1) * BLOCK, :]
            buffer[named[b] * capacity + rank] = jnp.where(at < length, rows, jnp.zeros_like(rows))

    pl.when(role == 0)(lambda: place(mine))
    pl.when(role == 1)(lambda: place(shifted))


def scores_of(q, keys):
    return lax.dot_general(q, keys, (((1,), (1,)), ((), ())), preferred_element_type=f32)


def weights_of(scores, highest):
    wide = jnp.concatenate([highest] * (scores.shape[1] // HD), axis=1)
    return jnp.exp2((scores - wide) * SCALE2).astype(bf16)


def stage(keys, values, first_half, second_half, parity):
    def fill(key_half, value_half):
        keys[...] = key_half[...]
        values[:, :HD] = value_half[...]

    pl.when(parity == 0)(lambda: fill(first_half, second_half))
    pl.when(parity == 1)(lambda: fill(second_half, first_half))
    values[:, HD:] = jnp.ones((values.shape[0], HD), bf16)


def cut(keys, values, length):
    for at in range(0, keys.shape[0], BLOCK):
        span = slice(at, at + BLOCK)

        @pl.when(length < at + BLOCK)
        def _():
            inside = at + lax.broadcasted_iota(jnp.int32, (BLOCK, HD), 0) < length
            first = jnp.broadcast_to(keys[0:1, :].astype(f32), (BLOCK, HD))
            keys[span, :] = jnp.where(inside, keys[span, :].astype(f32), first).astype(bf16)
            values[span, :HD] = jnp.where(inside, values[span, :HD].astype(f32), 0.0).astype(bf16)
            values[span, HD:] = jnp.where(inside, 1.0, 0.0).astype(bf16)


def step(state, scores, rows_of_values):
    highest = jnp.broadcast_to(jnp.max(scores, axis=1, keepdims=True), (scores.shape[0], HD))
    if state is None:
        return highest, rows_of_values(weights_of(scores, highest))
    old, summed = state
    highest = jnp.maximum(old, highest)
    factor = jnp.exp2((old - highest) * SCALE2)
    return highest, summed * jnp.concatenate([factor, factor], axis=1) + rows_of_values(weights_of(scores, highest))


def weighted(values):
    return lambda weights: jnp.dot(weights, values, preferred_element_type=f32)


def key_blocks(state, q, keys, values, first, last):
    for at in range(first, last, KEYS):
        state = step(state, scores_of(q, keys[at : at + KEYS, :]), weighted(values[at : at + KEYS, :]))
    return state


def finished(summed):
    return summed[:, :HD] / summed[:, HD:]


def prefill_rows(block, q, keys, values, length, out):
    at = block * ROWS
    diagonal = lax.broadcasted_iota(jnp.int32, (ROWS, KEYS), 1) <= lax.broadcasted_iota(jnp.int32, (ROWS, KEYS), 0)
    live = at + lax.broadcasted_iota(jnp.int32, (ROWS, 1), 0) < length
    for j in range(q.shape[1] // HD):
        rows = q[:, j * HD : (j + 1) * HD]
        state = key_blocks(None, rows, keys, values, 0, at)
        done = []
        for n in range(0, ROWS, KEYS):
            scores = jnp.where(diagonal[: ROWS - n], scores_of(rows[n:], keys[at + n : at + n + KEYS, :]), LOW)
            state = step(state, scores, weighted(values[at + n : at + n + KEYS, :]))
            done.append(finished(state[1][:KEYS]))
            state = tuple(x[KEYS:] for x in state)
        context = jnp.concatenate(done, axis=0)
        out[:, j * HD : (j + 1) * HD] = jnp.where(live, context, 0.0).astype(bf16)


def own_states(q, own_keys, own_values, bias, before):
    heads = q.shape[1] // HD
    states = []
    for n in range(0, ROWS, SPAN):
        span = slice(n, n + SPAN)
        rows = jnp.concatenate([q[span, j * HD : (j + 1) * HD] for j in range(heads)], axis=0)
        scores = scores_of(rows, own_keys[span, :]) + jnp.concatenate([bias[...]] * heads, axis=0)
        states.append(step(before(n), scores, weighted(own_values[span, :])))
    return states


def late_rows(q, keys, values, own_keys, own_values, bias, out):
    own = own_states(q, own_keys, own_values, bias, lambda n: None)
    for j in range(q.shape[1] // HD):
        span = slice(j * SPAN, (j + 1) * SPAN)
        state = tuple(jnp.concatenate([part[k][span] for part in own], axis=0) for k in range(2))
        state = key_blocks(state, q[:, j * HD : (j + 1) * HD], keys, values, 0, keys.shape[0])
        out[:, j * HD : (j + 1) * HD] = finished(state[1]).astype(bf16)


def early_rows(at, q, sums, tops, own_keys, own_values, bias, out):
    heads = q.shape[1] // HD

    def before(n):
        rows = slice(at + n, at + n + SPAN)
        return (
            jnp.concatenate([tops[rows, j * HD : (j + 1) * HD] for j in range(heads)], axis=0),
            jnp.concatenate([sums[rows, 2 * j * HD : 2 * (j + 1) * HD] for j in range(heads)], axis=0),
        )

    for n, (_, summed) in enumerate(own_states(q, own_keys, own_values, bias, before)):
        context = finished(summed).astype(bf16)
        for j in range(heads):
            out[n * SPAN : (n + 1) * SPAN, j * HD : (j + 1) * HD] = context[j * SPAN : (j + 1) * SPAN]


def first_kernel(lengths, q, shifted, shifted_across, acc, top, keys, values, sums, tops, sent):
    i = pl.program_id(0)
    role, parity = lax.axis_index("section"), lax.axis_index("heads") & 1
    length = lengths[lax.axis_index("rows")]
    heads = q.shape[1] // HD

    @pl.when((i == 0) & (role == 1))
    def _():
        stage(keys, values, shifted, shifted_across, parity)
        cut(keys, values, length)

    def saved(block, j):
        rows = pl.ds(block * ROWS, ROWS)
        wide, narrow = pl.ds(2 * j * HD, 2 * HD), pl.ds(j * HD, HD)
        return (
            pltpu.make_async_copy(sums.at[rows, wide], acc.at[rows, wide], sent.at[0, block, j]),
            pltpu.make_async_copy(tops.at[rows, narrow], top.at[rows, narrow], sent.at[1, block, j]),
        )

    for block in range(EARLY):

        @pl.when((role == 1) & (i == block))
        def _():
            rows = slice(block * ROWS, (block + 1) * ROWS)
            for j in range(heads):
                highest, summed = key_blocks(None, q[:, j * HD : (j + 1) * HD], keys, values, 0, keys.shape[0])
                sums[rows, 2 * j * HD : 2 * (j + 1) * HD] = summed
                tops[rows, j * HD : (j + 1) * HD] = highest
                for copy in saved(block, j):
                    copy.start()

    @pl.when((role == 1) & (i == EARLY - 1))
    def _():
        for block in range(EARLY):
            for j in range(heads):
                for copy in saved(block, j):
                    copy.wait()


def attend_kernel(
    lengths, q, mine, across, shifted, shifted_across, own_half, own_across, arrived, acc, top,
    ctx, pages, keys, values, own_keys, own_values, bias, sums, tops, loaded,
):
    i = pl.program_id(0)
    role, parity = lax.axis_index("section"), lax.axis_index("heads") & 1
    length = lengths[lax.axis_index("rows")]
    blocks = keys.shape[0] // ROWS
    late = blocks - EARLY
    pages[...] = arrived[...]
    loads = (
        pltpu.make_async_copy(acc, sums, loaded.at[0]),
        pltpu.make_async_copy(top, tops, loaded.at[1]),
    )

    @pl.when((i == 0) & (role == 0))
    def _():
        stage(keys, values, mine, across, parity)

    @pl.when((i == 0) & (role == 1))
    def _():
        for load in loads:
            load.start()
        stage(keys, values, shifted, shifted_across, parity)
        cut(keys, values, length)
        rows_at = lax.broadcasted_iota(jnp.int32, (SPAN, SPAN), 0)
        cols_at = lax.broadcasted_iota(jnp.int32, (SPAN, SPAN), 1)
        visible = (rows_at // STEPS == cols_at // STEPS) & (cols_at <= rows_at)
        bias[...] = jnp.where(visible, 0.0, LOW)

    for turn in range(blocks):

        @pl.when((role == 0) & (i == turn))
        def _():
            prefill_rows((turn + EARLY) % blocks, q, keys, values, length, ctx)

    @pl.when(role == 1)
    def _():
        stage(own_keys, own_values, own_half, own_across, parity)

        @pl.when(i == late)
        def _():
            for load in loads:
                load.wait()

        pl.when(i < late)(lambda: late_rows(q, keys, values, own_keys, own_values, bias, ctx))
        for block in range(EARLY):

            @pl.when(i == late + block)
            def _():
                early_rows(block * ROWS, q, sums, tops, own_keys, own_values, bias, ctx)


def shards(queries, keys_values, lengths, owners):
    rows_count, pairs = lax.axis_size("rows"), lax.axis_size("heads")
    seq_len, width = keys_values.shape[2:]
    block_count = seq_len // BLOCK
    capacity = 2 * block_count // rows_count
    mine = keys_values.reshape(seq_len, width)
    q = queries.reshape(seq_len, -1)
    q_width = q.shape[1]
    owners = owners.reshape(-1)

    def to_partner(value, section):
        return lax.ppermute(
            value, ("section", "heads"), [(section * pairs + h, pairs + (h ^ 1)) for h in range(pairs)]
        )

    own_across = to_partner(mine, 1)
    shifted_across = to_partner(mine, 0)
    shifted = lax.ppermute(mine, "section", [(0, 1)])
    whole = pl.BlockSpec(memory_space=pltpu.VMEM)
    smem = pl.BlockSpec(memory_space=pltpu.SMEM)
    params = pltpu.CompilerParams(vmem_limit_bytes=VMEM_LIMIT)
    buffer = pl.pallas_call(
        functools.partial(pages_kernel, block_count, capacity),
        in_specs=[smem, smem, whole, whole],
        out_specs=whole,
        out_shape=jax.ShapeDtypeStruct((rows_count * capacity, BLOCK, width), bf16),
        compiler_params=params,
        cost_estimate=pl.CostEstimate(flops=20 * 10**9, bytes_accessed=2**26, transcendentals=0),
        name="pages",
    )(lengths, owners, mine, shifted)
    arrived = lax.all_to_all(
        buffer.reshape(rows_count, capacity, BLOCK, width), "rows", split_axis=0, concat_axis=0, tiled=True
    )
    arrived = arrived.reshape(1, -1, BLOCK, width)

    shifted_across, _ = lax.optimization_barrier((shifted_across, buffer))
    across_mine = lax.ppermute(shifted_across, "section", [(1, 0)])

    def rows_of(width):
        return pl.BlockSpec((ROWS, width), lambda i: (i, 0))

    heads, blocks, early = q_width // HD, seq_len // ROWS, EARLY * ROWS
    anywhere = pl.BlockSpec(memory_space=pl.ANY)
    keys_scratch = [pltpu.VMEM((seq_len, HD), bf16), pltpu.VMEM((seq_len, 2 * HD), bf16)]
    state_scratch = [pltpu.VMEM((early, 2 * q_width), f32), pltpu.VMEM((early, q_width), f32)]
    acc, top = pl.pallas_call(
        first_kernel,
        grid=(EARLY,),
        in_specs=[smem, rows_of(q_width), whole, whole],
        out_specs=[anywhere, anywhere],
        out_shape=[
            jax.ShapeDtypeStruct((early, 2 * q_width), f32),
            jax.ShapeDtypeStruct((early, q_width), f32),
        ],
        scratch_shapes=[*keys_scratch, *state_scratch, pltpu.SemaphoreType.DMA((2, EARLY, heads))],
        compiler_params=params,
        cost_estimate=pl.CostEstimate(flops=FIRST_FLOPS, bytes_accessed=2**20, transcendentals=0),
        name="first_rows",
    )(lengths, q, shifted, shifted_across)

    def turned(width):
        return pl.BlockSpec((ROWS, width), lambda i: ((i + EARLY) % blocks, 0))

    slots = rows_count * capacity
    page_part = pl.BlockSpec((1, slots // blocks, BLOCK, width), lambda i: (0, i, 0, 0))
    context, kv_pages = pl.pallas_call(
        attend_kernel,
        grid=(blocks,),
        in_specs=[
            smem, turned(q_width), whole, whole, whole, whole, turned(width), turned(width), page_part, anywhere, anywhere,
        ],
        out_specs=[turned(q_width), page_part],
        out_shape=[
            jax.ShapeDtypeStruct((seq_len, q_width), bf16),
            jax.ShapeDtypeStruct((1, slots, BLOCK, width), bf16),
        ],
        scratch_shapes=[
            *keys_scratch,
            pltpu.VMEM((ROWS, HD), bf16),
            pltpu.VMEM((ROWS, 2 * HD), bf16),
            pltpu.VMEM((SPAN, SPAN), f32),
            *state_scratch,
            pltpu.SemaphoreType.DMA((2,)),
        ],
        compiler_params=params,
        cost_estimate=pl.CostEstimate(flops=11 * 10**9, bytes_accessed=2**20, transcendentals=0),
        name="attend",
    )(lengths, q, mine, across_mine, shifted, shifted_across, mine, own_across, arrived, acc, top)
    return (context.reshape(1, 1, seq_len, -1), kv_pages)


def solution(mesh):
    in_specs = (P("section", "rows", None, "heads"), P("section", "rows", None, "heads"), P(), P())
    out_specs = (P("section", "rows", None, "heads"), P("rows", None, None, "heads"))
    return jax.shard_map(shards, mesh=mesh, in_specs=in_specs, out_specs=out_specs, check_vma=False)
```
